512 devices in a mesh: dp: 32 (over z, x_lo, core), seq: 16 (over y, x_hi).
Axes of the slice: x: 4 (x_hi: 2, x_lo: 2; x = x_hi * 2 + x_lo), y: 8, z: 8, core: 2. Of those that a mesh axis runs over, the one named last changes fastest.
Arguments:
- query_saved: bfloat16 [32, 64, 32, 2048], P('dp', 'seq'), may hold values from -24 to 24
- key_saved: bfloat16 [32, 64, 32, 2048], P('dp', 'seq'), may hold values from -24 to 24
- value_saved: bfloat16 [32, 64, 32, 2048], P('dp', 'seq'), may hold values from -6 to 6
- grad_block: bfloat16 [32, 64, 32, 2048], P('dp', 'seq'), may hold values from -6 to 6
- out_weight: bfloat16 [2048, 2048], P('seq', 'dp'), may hold values from -0.125 to 0.125
Outputs:
- grad_query: bfloat16 [32, 64, 32, 2048], P('dp', 'seq')
- grad_key: bfloat16 [32, 64, 32, 2048], P('dp', 'seq')
- grad_value: bfloat16 [32, 64, 32, 2048], P('dp', 'seq')
The draws below stay inside these ranges and needn't reach their ends.
All inputs are finite; a program needn't handle non-finite values.
Results may differ from the reference program's by a relative error of at most 0.012.
The reference program's roundings to bfloat16 on the way (of `grad_attn`, `probs_low` and `grad_score`) count: a program that leaves them out, or rounds other values in their place, can miss the bound.
Values may be sent and summed in bfloat16 or wider, within the bound.
A program may use at most 64 MiB of HBM per device.

```python
import math
import jax
import jax.numpy as jnp
from jax import lax

D = 2048
HEADS = 16
HD = 128
FRAMES = 64
PATCHES = 32
CLIPS = 32


def draw_query_saved(key, part):
    key = jax.random.fold_in(key, 3)
    fresh = jnp.clip(jax.random.normal(key, (CLIPS, FRAMES, PATCHES, D), jnp.float32), -6.0, 6.0)
    return fresh.astype(jnp.bfloat16)


def draw_key_saved(key, part):
    key = jax.random.fold_in(key, 4)
    fresh = jnp.clip(jax.random.normal(key, (CLIPS, FRAMES, PATCHES, D), jnp.float32), -6.0, 6.0)
    return fresh.astype(jnp.bfloat16)


def shard_levels(rng, extent, pieces, smallest, largest):
    loudness = 1.0
    for axis_at, shards_of in pieces:
        steps = jax.random.uniform(jax.random.fold_in(jax.random.fold_in(rng, 6), axis_at), (shards_of,), jnp.float32, smallest / len(pieces), largest / len(pieces))
        loudness = loudness * jnp.repeat(jnp.exp(steps), extent[axis_at] // shards_of).reshape((-1,) + (1,) * (len(extent) - 1 - axis_at))
    return loudness


def normal_values(key, shape, scale, bound, cuts=(), kind=jnp.bfloat16):
    factor_of = shard_levels(key, shape, cuts, -0.22, 0.18) if cuts else 1.0
    array = jax.random.normal(key, shape, jnp.float32) * scale * factor_of
    return jnp.minimum(jnp.maximum(array, -bound), bound).astype(kind)


def setup_inputs(seed: int = 0) -> dict:
    key_list = jax.random.split(jax.random.key(seed), 6)
    query_saved = draw_query_saved(jax.random.fold_in(key_list[5], 71), 0)
    key_saved = draw_key_saved(jax.random.fold_in(key_list[5], 71), 0)
    value_saved = normal_values(key_list[2], (CLIPS, FRAMES, PATCHES, D), 1.0, 6.0, ((0, 32), (1, 16)))
    grad_block = normal_values(key_list[3], (CLIPS, FRAMES, PATCHES, D), 1.0, 6.0, ((0, 32), (1, 16)))
    out_weight = normal_values(key_list[4], (D, D), D ** -0.5, 0.125, ((0, 16), (1, 32)))
    return {"query_saved": query_saved, "key_saved": key_saved, "value_saved": value_saved, "grad_block": grad_block, "out_weight": out_weight}


def backward_local(query_in, key_in, value_in, grad_in):
    inv_root = 1.0 / math.sqrt(HD)
    frames_all = query_in.shape[0]
    query_wide = query_in.astype(jnp.float32)
    key_wide = key_in.astype(jnp.float32)
    value_wide = value_in.astype(jnp.float32)
    grad_wide = grad_in.astype(jnp.float32)
    scores = jnp.einsum('fxhd,gxhd->xhfg', query_wide, key_wide) * inv_root
    later = lax.broadcasted_iota(jnp.int32, (frames_all, frames_all), 0)
    earlier = lax.broadcasted_iota(jnp.int32, (frames_all, frames_all), 1)
    scores = jnp.where(later >= earlier, scores, -1e+30)
    row_max = lax.optimization_barrier(jnp.max(scores, axis=-1, keepdims=True))
    exponent = jnp.exp(scores - row_max)
    probable = exponent / lax.optimization_barrier(jnp.sum(exponent, axis=-1, keepdims=True))
    probs_low = probable.astype(jnp.bfloat16)
    probs_wide = probs_low.astype(jnp.float32)
    attended = jnp.einsum('xhfg,gxhd->fxhd', probs_wide, value_wide)
    row_delta = lax.optimization_barrier(jnp.sum(grad_wide * attended, axis=-1))
    grad_value = jnp.einsum('xhfg,fxhd->gxhd', probs_wide, grad_wide).astype(jnp.bfloat16)
    grad_prob = jnp.einsum('fxhd,gxhd->xhfg', grad_wide, value_wide)
    grad_score = (probable * (grad_prob - jnp.transpose(row_delta, (1, 2, 0))[..., None]) * inv_root).astype(jnp.bfloat16)
    score_wide = grad_score.astype(jnp.float32)
    grad_query = jnp.einsum('xhfg,gxhd->fxhd', score_wide, key_wide).astype(jnp.bfloat16)
    grad_key = jnp.einsum('xhfg,fxhd->gxhd', score_wide, query_wide).astype(jnp.bfloat16)
    return (grad_query, grad_key, grad_value)

def reference(query_saved, key_saved, value_saved, grad_block, out_weight):

    def per_clip(inputs):
        query_clip, key_clip, value_clip, grad_clip = inputs
        grad_attn = jnp.dot(grad_clip.reshape(FRAMES * PATCHES, D), out_weight.T, preferred_element_type=jnp.float32)
        grad_attn = grad_attn.astype(jnp.bfloat16).reshape(FRAMES, PATCHES, HEADS, HD)

        def split_heads(tensor):
            return tensor.reshape(FRAMES, PATCHES, HEADS, HD)
        results = backward_local(split_heads(query_clip), split_heads(key_clip), split_heads(value_clip), grad_attn)
        return tuple((item.reshape(FRAMES, PATCHES, D) for item in results))
    grad_query, grad_key, grad_value = lax.map(per_clip, (query_saved, key_saved, value_saved, grad_block))
    return (grad_query, grad_key, grad_value)
```

```python
import functools
import math

import jax
import jax.numpy as jnp
from jax import lax
from jax.experimental import pallas as pl
from jax.experimental.pallas import tpu as pltpu
from jax.sharding import PartitionSpec as P

HD = 128
F32 = jnp.float32
BF16 = jnp.bfloat16
MESH = pl.DeviceIdType.MESH
NT = (((1,), (1,)), ((), ()))
TN = (((0,), (0,)), ((), ()))
NN = (((1,), (0,)), ((), ()))


def dot(a, b, dims):
    return lax.dot_general(a, b, dims, preferred_element_type=F32)


def kernel(
    q, k, v, g, w, oq, ok, ov,
    rq, rk, rv, rg, gbuf, wt, ga, x32, qt, kt, vt, gt, pt, o32, so,
    in_send, in_recv, w_send, w_recv, z_send, z_recv, g_send, g_recv, ga_send, ga_recv, o_send, o_recv,
):
    dp, s = lax.axis_index("dp"), lax.axis_index("seq")
    z, u = lax.div(dp, 4), lax.rem(dp, 4)
    own_class = lax.div(s, 4)
    base = z * 4
    own = own_class == u
    inv_root = 1.0 / math.sqrt(HD)

    def ring(i, n):
        return lax.rem(i + n, n)

    up, down = ring(z + 1, 8) * 4 + u, ring(z - 1, 8) * 4 + u
    sibling = base + (u + 1 - 2 * lax.rem(u, 2))
    across = base + lax.rem(u + 2, 4)

    barrier = pltpu.get_barrier_semaphore()

    def greet(d, e):
        pl.semaphore_signal(barrier, inc=1, device_id=(d, e), device_id_type=MESH)

    def greet_seq(i, _):
        greet(dp, lax.rem(s + i, 16))
        return 0

    lax.fori_loop(1, 16, greet_seq, 0)

    def greet_group(i, _):
        t = lax.rem(s + i, 16)

        @pl.when(jnp.logical_or(base + lax.div(t, 4) != dp, 4 * u + lax.rem(t, 4) != s))
        def _():
            greet(base + lax.div(t, 4), 4 * u + lax.rem(t, 4))

        @pl.when(jnp.logical_or(own_class != u, t != s))
        def _():
            greet(base + own_class, t)

        return 0

    lax.fori_loop(0, 16, greet_group, 0)
    for d in (up, down, sibling, across):
        greet(d, s)
    pl.semaphore_wait(barrier, 51 - 2 * own.astype(jnp.int32))

    def w_rows():
        return wt.at[pl.ds(pl.multiple_of(dp * 64, 64), 64), pl.ds(pl.multiple_of(lax.rem(s, 4) * HD, HD), HD)]

    def w_copy(t):
        return pltpu.make_async_remote_copy(
            src_ref=w, dst_ref=w_rows(), send_sem=w_send, recv_sem=w_recv,
            device_id=(base + own_class, t), device_id_type=MESH)

    def w_go(i, _):
        t = lax.rem(s + i, 16)
        mine = jnp.logical_and(own, t == s)

        @pl.when(mine)
        def _():
            pltpu.make_async_copy(w, w_rows(), w_recv).start()

        @pl.when(jnp.logical_not(mine))
        def _():
            w_copy(t).start()

        return 0

    lax.fori_loop(0, 16, w_go, 0)

    pltpu.make_async_copy(g.at[0], gbuf.at[u], g_recv.at[0]).start()

    def g_copy(n, src, slot, d):
        return pltpu.make_async_remote_copy(
            src_ref=src, dst_ref=gbuf.at[slot], send_sem=g_send.at[n], recv_sem=g_recv.at[n],
            device_id=(d, s), device_id_type=MESH)

    to_across = g_copy(1, g.at[0], u, across)
    to_sibling = g_copy(2, g.at[0], u, sibling)
    across_slot = lax.rem(u + 2, 4)
    onward = g_copy(3, gbuf.at[across_slot], across_slot, sibling)
    to_across.start()
    to_sibling.start()

    pairs = ((q, rq), (k, rk), (v, rv))

    def lanes(h):
        return pl.ds(pl.multiple_of(h * HD, HD), HD)

    for n, (src, dst) in enumerate(pairs):
        pltpu.make_async_copy(src.at[0, :, :, lanes(s)], dst.at[s], in_recv.at[n]).start()

        def in_go(i, _, src=src, dst=dst, n=n):
            t = lax.rem(s + i, 16)
            pltpu.make_async_remote_copy(
                src_ref=src.at[0, :, :, lanes(t)], dst_ref=dst.at[s], send_sem=in_send.at[n], recv_sem=in_recv.at[n],
                device_id=(dp, t), device_id_type=MESH).start()
            return 0

        lax.fori_loop(1, 16, in_go, 0)

    def z_copy(way, h, step):
        slab = ring(z - step, 8) if way == 0 else ring(z + step, 8)
        rows = wt.at[pl.ds(pl.multiple_of(slab * 256 + h * 128, 128), 128)]
        return pltpu.make_async_remote_copy(
            src_ref=rows, dst_ref=rows, send_sem=z_send.at[way, h, step], recv_sem=z_recv.at[way, h, step],
            device_id=(up if way == 0 else down, s), device_id_type=MESH)

    def z_arrived(way, h, step):
        slab = ring(z - step - 1, 8) if way == 0 else ring(z + step + 1, 8)
        rows = wt.at[pl.ds(pl.multiple_of(slab * 256 + h * 128, 128), 128)]
        pltpu.make_async_remote_copy(
            src_ref=rows, dst_ref=rows, send_sem=z_send.at[way, h, step], recv_sem=z_recv.at[way, h, step],
            device_id=(up if way == 0 else down, s), device_id_type=MESH).wait_recv()

    hops = [(step, way, h) for step in range(4) for h in range(2) for way in range(2) if step < 3 or way == h]
    mine = wt.at[pl.ds(pl.multiple_of(z * 256, 256), 256)]
    pltpu.make_async_copy(mine, mine, w_recv).wait()
    for step, way, h in hops:
        if step:
            z_arrived(way, h, step - 1)
        z_copy(way, h, step).start()
        if (step, way, h) == (1, 1, 1):
            to_across.wait_recv()
            onward.start()
    for way, h in ((0, 1), (1, 0)):
        z_arrived(way, h, 2)
    for way in range(2):
        z_arrived(way, way, 3)

    pltpu.make_async_copy(g.at[0], gbuf.at[u], g_recv.at[0]).wait()
    to_sibling.wait_recv()
    onward.wait_recv()

    for half in range(2):
        acc = dot(gbuf[...].reshape(512, 2048), wt[:, half * 256 : half * 256 + 256], NN)
        acc = acc.astype(BF16)
        for j in range(2):
            ga[2 * half + j] = acc[:, j * HD : (j + 1) * HD].reshape(4, 4, 32, HD)

    def patches(c):
        return pl.ds(c * 16, 16)

    def ga_copy(c, t):
        b, j = lax.div(t, 4), lax.rem(t, 4)
        return pltpu.make_async_remote_copy(
            src_ref=ga.at[j, b, :, patches(c)], dst_ref=rg.at[s, :, patches(c)],
            send_sem=ga_send.at[c], recv_sem=ga_recv.at[c],
            device_id=(base + b, 4 * u + j), device_id_type=MESH)

    for c in range(2):

        def ga_go(i, _, c=c):
            t = lax.rem(s + i, 16)
            b, j = lax.div(t, 4), lax.rem(t, 4)
            mine = jnp.logical_and(b == u, 4 * u + j == s)

            @pl.when(mine)
            def _():
                pltpu.make_async_copy(ga.at[j, b, :, patches(c)], rg.at[s, :, patches(c)], ga_recv.at[c]).start()

            @pl.when(jnp.logical_not(mine))
            def _():
                ga_copy(c, t).start()

            return 0

        lax.fori_loop(0, 16, ga_go, 0)

    key_at = lax.broadcasted_iota(jnp.int32, (128, 128), 0)
    query_at = lax.broadcasted_iota(jnp.int32, (128, 128), 1)
    seen = jnp.logical_and(query_at >= key_at, (query_at >= 64) == (key_at >= 64))

    def widen(src):
        def step(i, _):
            x32[pl.ds(pl.multiple_of(i * 128, 128), 128)] = src[i].reshape(128, HD).astype(F32)
            return 0

        lax.fori_loop(0, 16, step, 0)

    def pair_of(p):
        a = x32[pl.ds(2 * p, 64, stride=32), :]
        b = x32[pl.ds(2 * p + 1, 64, stride=32), :]
        return jnp.concatenate([a, b], axis=0).astype(BF16)

    for n, (dst, out) in enumerate(((rq, qt), (rk, kt), (rv, vt))):
        pltpu.make_async_copy(dst, dst, in_recv.at[n]).wait()
        widen(dst)

        def regroup(p, _, out=out):
            out[p] = pair_of(p)
            return 0

        lax.fori_loop(0, 16, regroup, 0)

    def soft(p, _):
        scores = jnp.where(seen, dot(kt[p], qt[p], NT) * inv_root, -1e30)
        e = jnp.exp(scores - jnp.max(scores, axis=0, keepdims=True))
        pt[p] = e / jnp.sum(e, axis=0, keepdims=True)
        return 0

    lax.fori_loop(0, 16, soft, 0)

    outs = (oq, ok, ov)

    def out_copy(n, c, d):
        return pltpu.make_async_remote_copy(
            src_ref=so.at[n, d, :, patches(c)], dst_ref=outs[n].at[0, :, patches(c), lanes(s)],
            send_sem=o_send.at[n], recv_sem=o_recv.at[n],
            device_id=(dp, d), device_id_type=MESH)

    for c in range(2):
        part = rg.at[:, :, patches(c)]
        pltpu.make_async_copy(part, part, ga_recv.at[c]).wait()

        def widen_g(i, _, c=c):
            for f in range(4):
                x32[pl.ds(pl.multiple_of(i * 128 + f * 32 + c * 16, 16), 16)] = rg[i, f, c * 16 : c * 16 + 16].astype(F32)
            return 0

        lax.fori_loop(0, 16, widen_g, 0)

        def grads(p, _):
            gp, vp, prob = pair_of(p), vt[p], pt[p]
            low = prob.astype(BF16)
            grad_prob = dot(vp, gp, NT)
            delta = jnp.sum(low.astype(F32) * grad_prob, axis=0, keepdims=True)
            ds = (prob * (grad_prob - delta) * inv_root).astype(BF16)
            for n, val in ((2, dot(low, gp, NN)), (1, dot(ds, qt[p], NN)), (0, dot(ds, kt[p], TN))):
                o32[n, pl.ds(2 * p, 64, stride=32), :] = val[:64]
                o32[n, pl.ds(2 * p + 1, 64, stride=32), :] = val[64:]
            return 0

        lax.fori_loop(c * 8, c * 8 + 8, grads, 0)

        for n in range(3):

            def narrow(i, _, n=n, c=c):
                for f in range(4):
                    rows = pl.ds(pl.multiple_of(i * 128 + f * 32 + c * 16, 16), 16)
                    so[n, i, f, c * 16 : c * 16 + 16] = o32[n, rows, :].astype(BF16)
                return 0

            lax.fori_loop(0, 16, narrow, 0)
            pltpu.make_async_copy(
                so.at[n, s, :, patches(c)], outs[n].at[0, :, patches(c), lanes(s)], o_recv.at[n]).start()

            def out_go(i, _, n=n, c=c):
                out_copy(n, c, lax.rem(s + i, 16)).start()
                return 0

            lax.fori_loop(1, 16, out_go, 0)

    for n, (src, dst) in enumerate(pairs):
        part = src.at[0, :, :, pl.ds(0, 15 * HD)]
        pltpu.make_async_copy(part, part, in_send.at[n]).wait()
    for step, way, h in hops:
        z_copy(way, h, step).wait_send()
    for copy in (to_across, to_sibling, onward):
        copy.wait_send()

    def drain(ref, sem):
        pltpu.make_async_copy(ref, ref, sem).wait()

    @pl.when(own)
    def _():
        drain(wt.at[pl.ds(0, 240)], w_send)
        for c in range(2):
            drain(rg.at[pl.ds(0, 15), :, patches(c)], ga_send.at[c])

    @pl.when(jnp.logical_not(own))
    def _():
        drain(wt.at[pl.ds(0, 256)], w_send)
        for c in range(2):
            drain(rg.at[:, :, patches(c)], ga_send.at[c])

    for n in range(3):
        drain(so.at[n, pl.ds(0, 15)], o_send.at[n])
        drain(outs[n], o_recv.at[n])


def body(query_saved, key_saved, value_saved, grad_block, out_weight):
    shape = jax.ShapeDtypeStruct(query_saved.shape, BF16)
    anywhere = pl.BlockSpec(memory_space=pl.ANY)
    dma = pltpu.SemaphoreType.DMA
    return pl.pallas_call(
        kernel,
        out_shape=(shape, shape, shape),
        in_specs=[anywhere] * 5,
        out_specs=(anywhere,) * 3,
        scratch_shapes=[
            *[pltpu.VMEM((16, 4, 32, HD), BF16)] * 4,
            pltpu.VMEM((4, 4, 32, 2048), BF16),
            pltpu.VMEM((2048, 512), BF16),
            pltpu.VMEM((4, 4, 4, 32, HD), BF16),
            pltpu.VMEM((2048, HD), F32),
            *[pltpu.VMEM((16, 128, HD), BF16)] * 4,
            pltpu.VMEM((16, 128, 128), F32),
            pltpu.VMEM((3, 2048, HD), F32),
            pltpu.VMEM((3, 16, 4, 32, HD), BF16),
            dma((3,)), dma((3,)),
            dma, dma,
            dma((2, 2, 4)), dma((2, 2, 4)),
            dma((4,)), dma((4,)),
            dma((2,)), dma((2,)),
            dma((3,)), dma((3,)),
        ],
        compiler_params=pltpu.CompilerParams(
            collective_id=0, has_side_effects=True, vmem_limit_bytes=48 * 1024 * 1024),
    )(query_saved, key_saved, value_saved, grad_block, out_weight.T)


def solution(mesh):
    spec = P("dp", "seq", None, None)
    return jax.shard_map(
        body, mesh=mesh, in_specs=(spec, spec, spec, spec, P("seq", "dp")), out_specs=(spec, spec, spec), check_vma=False)
```

```python
import functools
import math

import jax
import jax.numpy as jnp
from jax import lax
from jax.experimental import pallas as pl
from jax.experimental.pallas import tpu as pltpu
from jax.sharding import PartitionSpec as P

HD = 128
F32 = jnp.float32
BF16 = jnp.bfloat16
MESH = pl.DeviceIdType.MESH
NT = (((1,), (1,)), ((), ()))
TN = (((0,), (0,)), ((), ()))
NN = (((1,), (0,)), ((), ()))


def dot(a, b, dims):
    return lax.dot_general(a, b, dims, preferred_element_type=F32)


def kernel(
    q, k, v, g, w, oq, ok, ov,
    rq, rk, rv, rg, gbuf, wt, acc, ga, x32, qt, kt, vt, gt, pt, o32, so,
    in_send, in_recv, w_send, w_recv, z_send, z_recv, g_send, g_recv, ga_send, ga_recv, o_send, o_recv,
):
    dp, s = lax.axis_index("dp"), lax.axis_index("seq")
    z, u = lax.div(dp, 4), lax.rem(dp, 4)
    own_class = lax.rem(s, 2) * 2 + lax.rem(lax.div(s, 2), 2)
    place = lax.div(s, 4)

    def head(j):
        return 4 * j + 2 * lax.rem(u, 2) + lax.div(u, 2)

    base = z * 4
    own = own_class == u
    inv_root = 1.0 / math.sqrt(HD)

    def ring(i, n):
        return lax.rem(i + n, n)

    up, down = ring(z + 1, 8) * 4 + u, ring(z - 1, 8) * 4 + u
    sibling = base + (u + 1 - 2 * lax.rem(u, 2))
    across = base + lax.rem(u + 2, 4)

    barrier = pltpu.get_barrier_semaphore()

    def greet(d, e):
        pl.semaphore_signal(barrier, inc=1, device_id=(d, e), device_id_type=MESH)

    def greet_seq(i, _):
        greet(dp, lax.rem(s + i, 16))
        return 0

    lax.fori_loop(1, 16, greet_seq, 0)

    def greet_group(i, _):
        t = lax.rem(s + i, 16)

        @pl.when(jnp.logical_or(base + lax.div(t, 4) != dp, head(lax.rem(t, 4)) != s))
        def _():
            greet(base + lax.div(t, 4), head(lax.rem(t, 4)))

        @pl.when(jnp.logical_or(own_class != u, t != s))
        def _():
            greet(base + own_class, t)

        return 0

    lax.fori_loop(0, 16, greet_group, 0)
    for d in (up, down, sibling, across):
        greet(d, s)
    pl.semaphore_wait(barrier, 51 - 2 * own.astype(jnp.int32))

    def w_rows():
        return wt.at[pl.ds(pl.multiple_of(dp * 64, 64), 64), pl.ds(pl.multiple_of(place * HD, HD), HD)]

    def w_copy(t):
        return pltpu.make_async_remote_copy(
            src_ref=w, dst_ref=w_rows(), send_sem=w_send, recv_sem=w_recv,
            device_id=(base + own_class, t), device_id_type=MESH)

    def w_go(i, _):
        t = lax.rem(s + i, 16)
        mine = jnp.logical_and(own, t == s)

        @pl.when(mine)
        def _():
            pltpu.make_async_copy(w, w_rows(), w_recv).start()

        @pl.when(jnp.logical_not(mine))
        def _():
            w_copy(t).start()

        return 0

    lax.fori_loop(0, 16, w_go, 0)

    pltpu.make_async_copy(g.at[0], gbuf.at[u], g_recv.at[0]).start()

    def g_copy(n, src, slot, d):
        return pltpu.make_async_remote_copy(
            src_ref=src, dst_ref=gbuf.at[slot], send_sem=g_send.at[n], recv_sem=g_recv.at[n],
            device_id=(d, s), device_id_type=MESH)

    to_across = g_copy(1, g.at[0], u, across)
    to_sibling = g_copy(2, g.at[0], u, sibling)
    across_slot = lax.rem(u + 2, 4)
    onward = g_copy(3, gbuf.at[across_slot], across_slot, sibling)
    to_across.start()
    to_sibling.start()

    pairs = ((q, rq), (k, rk), (v, rv))

    def lanes(h):
        return pl.ds(pl.multiple_of(h * HD, HD), HD)

    for n, (src, dst) in enumerate(pairs):
        pltpu.make_async_copy(src.at[0, :, :, lanes(s)], dst.at[s], in_recv.at[n]).start()

        def in_go(i, _, src=src, dst=dst, n=n):
            t = lax.rem(s + i, 16)
            pltpu.make_async_remote_copy(
                src_ref=src.at[0, :, :, lanes(t)], dst_ref=dst.at[s], send_sem=in_send.at[n], recv_sem=in_recv.at[n],
                device_id=(dp, t), device_id_type=MESH).start()
            return 0

        lax.fori_loop(1, 16, in_go, 0)

    def z_copy(way, h, step):
        slab = ring(z - step, 8) if way == 0 else ring(z + step, 8)
        rows = wt.at[pl.ds(pl.multiple_of(slab * 256 + h * 128, 128), 128)]
        return pltpu.make_async_remote_copy(
            src_ref=rows, dst_ref=rows, send_sem=z_send.at[way, h, step], recv_sem=z_recv.at[way, h, step],
            device_id=(up if way == 0 else down, s), device_id_type=MESH)

    def z_arrived(way, h, step):
        slab = ring(z - step - 1, 8) if way == 0 else ring(z + step + 1, 8)
        rows = wt.at[pl.ds(pl.multiple_of(slab * 256 + h * 128, 128), 128)]
        pltpu.make_async_remote_copy(
            src_ref=rows, dst_ref=rows, send_sem=z_send.at[way, h, step], recv_sem=z_recv.at[way, h, step],
            device_id=(up if way == 0 else down, s), device_id_type=MESH).wait_recv()

    hops = [(step, way, h) for step in range(4) for h in range(2) for way in range(2) if step < 3 or way == h]
    mine = wt.at[pl.ds(pl.multiple_of(z * 256, 256), 256)]
    pltpu.make_async_copy(mine, mine, w_recv).wait()

    def project(slab, first=False):
        cols = pl.ds(pl.multiple_of(slab * 256, 256), 256)

        def step(half, _):
            part = dot(
                gbuf[:, :, :, cols].reshape(512, 256),
                wt[cols, pl.ds(pl.multiple_of(half * 256, 256), 256)], NN)
            acc[half] = part if first else acc[half] + part
            return 0

        lax.fori_loop(0, 2, step, 0)

    ready = [0]
    for step, way, h in hops:
        if step:
            z_arrived(way, h, step - 1)
        z_copy(way, h, step).start()
        if (step, way, h) == (1, 1, 1):
            to_across.wait_recv()
            onward.start()
        if (step, way, h) == (2, 0, 0):
            pltpu.make_async_copy(g.at[0], gbuf.at[u], g_recv.at[0]).wait()
            to_sibling.wait_recv()
            onward.wait_recv()
        if step in (1, 2) and h == 1:
            ready.append(step if way else -step)
        if step >= 2 and ready:
            slab = ready.pop(0)
            project(ring(z + slab, 8), first=slab == 0)
    for way, h in ((0, 1), (1, 0)):
        z_arrived(way, h, 2)
    ready += [-3, 3]
    for slab in ready:
        project(ring(z + slab, 8))
    for way in range(2):
        z_arrived(way, way, 3)
    project(ring(z + 4, 8))

    for half in range(2):
        val = acc[half].astype(BF16)
        for j in range(2):
            ga[2 * half + j] = val[:, j * HD : (j + 1) * HD].reshape(4, 4, 32, HD)

    def patches(c):
        return pl.ds(c * 16, 16)

    def ga_copy(c, t):
        b, j = lax.div(t, 4), lax.rem(t, 4)
        return pltpu.make_async_remote_copy(
            src_ref=ga.at[j, b, :, patches(c)], dst_ref=rg.at[s, :, patches(c)],
            send_sem=ga_send.at[c], recv_sem=ga_recv.at[c],
            device_id=(base + b, head(j)), device_id_type=MESH)

    for c in range(2):

        def ga_go(i, _, c=c):
            t = lax.rem(s + i, 16)
            b, j = lax.div(t, 4), lax.rem(t, 4)
            mine = jnp.logical_and(b == u, head(j) == s)

            @pl.when(mine)
            def _():
                pltpu.make_async_copy(ga.at[j, b, :, patches(c)], rg.at[s, :, patches(c)], ga_recv.at[c]).start()

            @pl.when(jnp.logical_not(mine))
            def _():
                ga_copy(c, t).start()

            return 0

        lax.fori_loop(0, 16, ga_go, 0)

    key_at = lax.broadcasted_iota(jnp.int32, (128, 128), 0)
    query_at = lax.broadcasted_iota(jnp.int32, (128, 128), 1)
    seen = jnp.logical_and(query_at >= key_at, (query_at >= 64) == (key_at >= 64))

    def widen(src):
        def step(i, _):
            x32[pl.ds(pl.multiple_of(i * 128, 128), 128)] = src[i].reshape(128, HD).astype(F32)
            return 0

        lax.fori_loop(0, 16, step, 0)

    def pair_of(p):
        a = x32[pl.ds(2 * p, 64, stride=32), :]
        b = x32[pl.ds(2 * p + 1, 64, stride=32), :]
        return jnp.concatenate([a, b], axis=0).astype(BF16)

    for n, (dst, out) in enumerate(((rq, qt), (rk, kt), (rv, vt))):
        pltpu.make_async_copy(dst, dst, in_recv.at[n]).wait()
        widen(dst)

        def regroup(p, _, out=out):
            out[p] = pair_of(p)
            return 0

        lax.fori_loop(0, 16, regroup, 0)

    def soft(p, _):
        scores = jnp.where(seen, dot(kt[p], qt[p], NT) * inv_root, -1e30)
        e = jnp.exp(scores - jnp.max(scores, axis=0, keepdims=True))
        pt[p] = e / jnp.sum(e, axis=0, keepdims=True)
        return 0

    lax.fori_loop(0, 16, soft, 0)

    outs = (oq, ok, ov)

    def out_copy(n, c, d):
        return pltpu.make_async_remote_copy(
            src_ref=so.at[n, d, :, patches(c)], dst_ref=outs[n].at[0, :, patches(c), lanes(s)],
            send_sem=o_send.at[n], recv_sem=o_recv.at[n],
            device_id=(dp, d), device_id_type=MESH)

    for c in range(2):
        part = rg.at[:, :, patches(c)]
        pltpu.make_async_copy(part, part, ga_recv.at[c]).wait()

        def widen_g(i, _, c=c):
            for f in range(4):
                x32[pl.ds(pl.multiple_of(i * 128 + f * 32 + c * 16, 16), 16)] = rg[i, f, c * 16 : c * 16 + 16].astype(F32)
            return 0

        lax.fori_loop(0, 16, widen_g, 0)

        def grads(p, _):
            gp, vp, prob = pair_of(p), vt[p], pt[p]
            low = prob.astype(BF16)
            grad_prob = dot(vp, gp, NT)
            delta = jnp.sum(low.astype(F32) * grad_prob, axis=0, keepdims=True)
            ds = (prob * (grad_prob - delta) * inv_root).astype(BF16)
            for n, val in ((2, dot(low, gp, NN)), (1, dot(ds, qt[p], NN)), (0, dot(ds, kt[p], TN))):
                o32[n, pl.ds(2 * p, 64, stride=32), :] = val[:64]
                o32[n, pl.ds(2 * p + 1, 64, stride=32), :] = val[64:]
            return 0

        lax.fori_loop(c * 8, c * 8 + 8, grads, 0)

        for n in range(3):

            def narrow(i, _, n=n, c=c):
                for f in range(4):
                    rows = pl.ds(pl.multiple_of(i * 128 + f * 32 + c * 16, 16), 16)
                    so[n, i, f, c * 16 : c * 16 + 16] = o32[n, rows, :].astype(BF16)
                return 0

            lax.fori_loop(0, 16, narrow, 0)
            pltpu.make_async_copy(
                so.at[n, s, :, patches(c)], outs[n].at[0, :, patches(c), lanes(s)], o_recv.at[n]).start()

            def out_go(i, _, n=n, c=c):
                out_copy(n, c, lax.rem(s + i, 16)).start()
                return 0

            lax.fori_loop(1, 16, out_go, 0)

    for n, (src, dst) in enumerate(pairs):
        part = src.at[0, :, :, pl.ds(0, 15 * HD)]
        pltpu.make_async_copy(part, part, in_send.at[n]).wait()
    for step, way, h in hops:
        z_copy(way, h, step).wait_send()
    for copy in (to_across, to_sibling, onward):
        copy.wait_send()

    def drain(ref, sem):
        pltpu.make_async_copy(ref, ref, sem).wait()

    @pl.when(own)
    def _():
        drain(wt.at[pl.ds(0, 240)], w_send)
        for c in range(2):
            drain(rg.at[pl.ds(0, 15), :, patches(c)], ga_send.at[c])

    @pl.when(jnp.logical_not(own))
    def _():
        drain(wt.at[pl.ds(0, 256)], w_send)
        for c in range(2):
            drain(rg.at[:, :, patches(c)], ga_send.at[c])

    for n in range(3):
        drain(so.at[n, pl.ds(0, 15)], o_send.at[n])
        drain(outs[n], o_recv.at[n])


def body(query_saved, key_saved, value_saved, grad_block, out_weight):
    shape = jax.ShapeDtypeStruct(query_saved.shape, BF16)
    anywhere = pl.BlockSpec(memory_space=pl.ANY)
    dma = pltpu.SemaphoreType.DMA
    return pl.pallas_call(
        kernel,
        out_shape=(shape, shape, shape),
        in_specs=[anywhere] * 5,
        out_specs=(anywhere,) * 3,
        scratch_shapes=[
            *[pltpu.VMEM((16, 4, 32, HD), BF16)] * 4,
            pltpu.VMEM((4, 4, 32, 2048), BF16),
            pltpu.VMEM((2048, 512), BF16),
            pltpu.VMEM((2, 512, 256), F32),
            pltpu.VMEM((4, 4, 4, 32, HD), BF16),
            pltpu.VMEM((2048, HD), F32),
            *[pltpu.VMEM((16, 128, HD), BF16)] * 4,
            pltpu.VMEM((16, 128, 128), F32),
            pltpu.VMEM((3, 2048, HD), F32),
            pltpu.VMEM((3, 16, 4, 32, HD), BF16),
            dma((3,)), dma((3,)),
            dma, dma,
            dma((2, 2, 4)), dma((2, 2, 4)),
            dma((4,)), dma((4,)),
            dma((2,)), dma((2,)),
            dma((3,)), dma((3,)),
        ],
        compiler_params=pltpu.CompilerParams(
            collective_id=0, has_side_effects=True, vmem_limit_bytes=60 * 1024 * 1024),
    )(query_saved, key_saved, value_saved, grad_block, out_weight.T)


def solution(mesh):
    spec = P("dp", "seq", None, None)
    return jax.shard_map(
        body, mesh=mesh, in_specs=(spec, spec, spec, spec, P("seq", "dp")), out_specs=(spec, spec, spec), check_vma=False)
```

```python
import functools
import math

import jax
import jax.numpy as jnp
from jax import lax
from jax.experimental import pallas as pl
from jax.experimental.pallas import tpu as pltpu
from jax.sharding import PartitionSpec as P

HD = 128
F32 = jnp.float32
BF16 = jnp.bfloat16
MESH = pl.DeviceIdType.MESH
NT = (((1,), (1,)), ((), ()))
TN = (((0,), (0,)), ((), ()))
NN = (((1,), (0,)), ((), ()))


def dot(a, b, dims):
    return lax.dot_general(a, b, dims, preferred_element_type=F32)


def kernel(
    q, k, v, g, w, oq, ok, ov,
    rq, rk, rv, rg, gbuf, wt, acc, ga, x32, qt, kt, vt, gt, pt, o32, so,
    in_send, in_recv, w_send, w_recv, z_send, z_recv, g_send, g_recv, ga_send, ga_recv, o_send, o_recv,
):
    dp, s = lax.axis_index("dp"), lax.axis_index("seq")
    z, u = lax.div(dp, 4), lax.rem(dp, 4)
    own_class = lax.rem(s, 2) * 2 + lax.rem(lax.div(s, 2), 2)
    place = lax.div(s, 4)

    def head(j):
        return 4 * j + 2 * lax.rem(u, 2) + lax.div(u, 2)

    base = z * 4
    own = own_class == u
    inv_root = 1.0 / math.sqrt(HD)

    def ring(i, n):
        return lax.rem(i + n, n)

    up, down = ring(z + 1, 8) * 4 + u, ring(z - 1, 8) * 4 + u
    sibling = base + (u + 1 - 2 * lax.rem(u, 2))
    across = base + lax.rem(u + 2, 4)

    barrier = pltpu.get_barrier_semaphore()

    def greet(d, e):
        pl.semaphore_signal(barrier, inc=1, device_id=(d, e), device_id_type=MESH)

    def greet_seq(i, _):
        greet(dp, lax.rem(s + i, 16))
        return 0

    lax.fori_loop(1, 16, greet_seq, 0)

    def greet_group(i, _):
        t = lax.rem(s + i, 16)

        @pl.when(jnp.logical_or(base + lax.div(t, 4) != dp, head(lax.rem(t, 4)) != s))
        def _():
            greet(base + lax.div(t, 4), head(lax.rem(t, 4)))

        @pl.when(jnp.logical_or(own_class != u, t != s))
        def _():
            greet(base + own_class, t)

        return 0

    lax.fori_loop(0, 16, greet_group, 0)
    for d in (up, down, sibling, across):
        greet(d, s)
    pl.semaphore_wait(barrier, 51 - 2 * own.astype(jnp.int32))

    def w_rows():
        return wt.at[pl.ds(pl.multiple_of(dp * 64, 64), 64), pl.ds(pl.multiple_of(place * HD, HD), HD)]

    def w_copy(t):
        return pltpu.make_async_remote_copy(
            src_ref=w, dst_ref=w_rows(), send_sem=w_send, recv_sem=w_recv,
            device_id=(base + own_class, t), device_id_type=MESH)

    def w_go(i, _):
        t = lax.rem(s + i, 16)
        mine = jnp.logical_and(own, t == s)

        @pl.when(mine)
        def _():
            pltpu.make_async_copy(w, w_rows(), w_recv).start()

        @pl.when(jnp.logical_not(mine))
        def _():
            w_copy(t).start()

        return 0

    lax.fori_loop(0, 16, w_go, 0)

    pltpu.make_async_copy(g.at[0], gbuf.at[u], g_recv.at[0]).start()

    def g_copy(n, src, slot, d):
        return pltpu.make_async_remote_copy(
            src_ref=src, dst_ref=gbuf.at[slot], send_sem=g_send.at[n], recv_sem=g_recv.at[n],
            device_id=(d, s), device_id_type=MESH)

    to_across = g_copy(1, g.at[0], u, across)
    to_sibling = g_copy(2, g.at[0], u, sibling)
    across_slot = lax.rem(u + 2, 4)
    onward = g_copy(3, gbuf.at[across_slot], across_slot, sibling)
    to_across.start()
    to_sibling.start()

    pairs = ((q, rq), (k, rk), (v, rv))

    def lanes(h):
        return pl.ds(pl.multiple_of(h * HD, HD), HD)

    for n, (src, dst) in enumerate(pairs):
        pltpu.make_async_copy(src.at[0, :, :, lanes(s)], dst.at[s], in_recv.at[n]).start()

        def in_go(i, _, src=src, dst=dst, n=n):
            t = lax.rem(s + i, 16)
            pltpu.make_async_remote_copy(
                src_ref=src.at[0, :, :, lanes(t)], dst_ref=dst.at[s], send_sem=in_send.at[n], recv_sem=in_recv.at[n],
                device_id=(dp, t), device_id_type=MESH).start()
            return 0

        lax.fori_loop(1, 16, in_go, 0)

    def z_copy(way, h, step):
        slab = ring(z - step, 8) if way == 0 else ring(z + step, 8)
        rows = wt.at[pl.ds(pl.multiple_of(slab * 256 + h * 128, 128), 128)]
        return pltpu.make_async_remote_copy(
            src_ref=rows, dst_ref=rows, send_sem=z_send.at[way, h, step], recv_sem=z_recv.at[way, h, step],
            device_id=(up if way == 0 else down, s), device_id_type=MESH)

    def z_arrived(way, h, step):
        slab = ring(z - step - 1, 8) if way == 0 else ring(z + step + 1, 8)
        rows = wt.at[pl.ds(pl.multiple_of(slab * 256 + h * 128, 128), 128)]
        pltpu.make_async_remote_copy(
            src_ref=rows, dst_ref=rows, send_sem=z_send.at[way, h, step], recv_sem=z_recv.at[way, h, step],
            device_id=(up if way == 0 else down, s), device_id_type=MESH).wait_recv()

    hops = [(step, way, h) for step in range(4) for h in range(2) for way in range(2) if step < 3 or way == h]
    mine = wt.at[pl.ds(pl.multiple_of(z * 256, 256), 256)]
    pltpu.make_async_copy(mine, mine, w_recv).wait()

    def project(slab, first=False):
        cols = pl.ds(pl.multiple_of(slab * 256, 256), 256)

        def step(half, _):
            part = dot(
                gbuf[:, :, :, cols].reshape(512, 256),
                wt[cols, pl.ds(pl.multiple_of(half * 256, 256), 256)], NN)
            acc[half] = part if first else acc[half] + part
            return 0

        lax.fori_loop(0, 2, step, 0)

    ready = [0]
    for step, way, h in hops:
        if step:
            z_arrived(way, h, step - 1)
        z_copy(way, h, step).start()
        if (step, way, h) == (1, 1, 1):
            to_across.wait_recv()
            onward.start()
        if (step, way, h) == (2, 0, 0):
            pltpu.make_async_copy(g.at[0], gbuf.at[u], g_recv.at[0]).wait()
            to_sibling.wait_recv()
            onward.wait_recv()
        if step in (1, 2) and h == 1:
            ready.append(step if way else -step)
        if step >= 2 and ready:
            slab = ready.pop(0)
            project(ring(z + slab, 8), first=slab == 0)
    for way, h in ((0, 1), (1, 0)):
        z_arrived(way, h, 2)
    ready += [-3, 3]
    for slab in ready:
        project(ring(z + slab, 8))
    for way in range(2):
        z_arrived(way, way, 3)
    project(ring(z + 4, 8))

    for half in range(2):
        val = acc[half].astype(BF16)
        for j in range(2):
            ga[2 * half + j] = val[:, j * HD : (j + 1) * HD].reshape(4, 4, 32, HD)

    def patches(c):
        return pl.ds(c * 16, 16)

    def ga_copy(c, t):
        b, j = lax.div(t, 4), lax.rem(t, 4)
        return pltpu.make_async_remote_copy(
            src_ref=ga.at[j, b, :, patches(c)], dst_ref=rg.at[s, :, patches(c)],
            send_sem=ga_send.at[c], recv_sem=ga_recv.at[c],
            device_id=(base + b, head(j)), device_id_type=MESH)

    for c in range(2):

        def ga_go(i, _, c=c):
            t = lax.rem(s + i, 16)
            b, j = lax.div(t, 4), lax.rem(t, 4)
            mine = jnp.logical_and(b == u, head(j) == s)

            @pl.when(mine)
            def _():
                pltpu.make_async_copy(ga.at[j, b, :, patches(c)], rg.at[s, :, patches(c)], ga_recv.at[c]).start()

            @pl.when(jnp.logical_not(mine))
            def _():
                ga_copy(c, t).start()

            return 0

        lax.fori_loop(0, 16, ga_go, 0)

    key_at = lax.broadcasted_iota(jnp.int32, (128, 128), 0)
    query_at = lax.broadcasted_iota(jnp.int32, (128, 128), 1)
    seen = jnp.logical_and(query_at >= key_at, (query_at >= 64) == (key_at >= 64))

    def widen(src):
        def step(i, _):
            x32[pl.ds(pl.multiple_of(i * 128, 128), 128)] = src[i].reshape(128, HD).astype(F32)
            return 0

        lax.fori_loop(0, 16, step, 0)

    def pair_of(p):
        a = x32[pl.ds(2 * p, 64, stride=32), :]
        b = x32[pl.ds(2 * p + 1, 64, stride=32), :]
        return jnp.concatenate([a, b], axis=0).astype(BF16)

    for n, (dst, out) in enumerate(((rq, qt), (rk, kt), (rv, vt))):
        pltpu.make_async_copy(dst, dst, in_recv.at[n]).wait()
        widen(dst)

        def regroup(p, _, out=out):
            out[p] = pair_of(p)
            return 0

        lax.fori_loop(0, 16, regroup, 0)

    def soft(p, _):
        scores = jnp.where(seen, dot(kt[p], qt[p], NT) * inv_root, -1e30)
        e = jnp.exp(scores - jnp.max(scores, axis=0, keepdims=True))
        pt[p] = e / jnp.sum(e, axis=0, keepdims=True)
        return 0

    lax.fori_loop(0, 16, soft, 0)

    outs = (oq, ok, ov)

    def out_copy(n, c, d):
        return pltpu.make_async_remote_copy(
            src_ref=so.at[n, d, :, patches(c)], dst_ref=outs[n].at[0, :, patches(c), lanes(s)],
            send_sem=o_send.at[n], recv_sem=o_recv.at[n],
            device_id=(dp, d), device_id_type=MESH)

    for c in range(2):
        part = rg.at[:, :, patches(c)]
        pltpu.make_async_copy(part, part, ga_recv.at[c]).wait()

        def widen_g(i, _, c=c):
            for f in range(4):
                x32[pl.ds(pl.multiple_of(i * 128 + f * 32 + c * 16, 16), 16)] = rg[i, f, c * 16 : c * 16 + 16].astype(F32)
            return 0

        lax.fori_loop(0, 16, widen_g, 0)

        def grads(p, _):
            gp, vp, prob = pair_of(p), vt[p], pt[p]
            low = prob.astype(BF16)
            grad_prob = dot(vp, gp, NT)
            delta = jnp.sum(low.astype(F32) * grad_prob, axis=0, keepdims=True)
            ds = (prob * (grad_prob - delta) * inv_root).astype(BF16)
            for n, val in ((2, dot(low, gp, NN)), (1, dot(ds, qt[p], NN)), (0, dot(ds, kt[p], TN))):
                o32[n, pl.ds(2 * p, 64, stride=32), :] = val[:64]
                o32[n, pl.ds(2 * p + 1, 64, stride=32), :] = val[64:]
            return 0

        lax.fori_loop(c * 8, c * 8 + 8, grads, 0)

        for n in range(3):

            def narrow(i, _, n=n, c=c):
                for f in range(4):
                    rows = pl.ds(pl.multiple_of(i * 128 + f * 32 + c * 16, 16), 16)
                    so[n, i, f, c * 16 : c * 16 + 16] = o32[n, rows, :].astype(BF16)
                return 0

            lax.fori_loop(0, 16, narrow, 0)
            pltpu.make_async_copy(
                so.at[n, s, :, patches(c)], outs[n].at[0, :, patches(c), lanes(s)], o_recv.at[n]).start()

            def out_go(i, _, n=n, c=c):
                out_copy(n, c, lax.rem(s + i, 16)).start()
                return 0

            lax.fori_loop(1, 16, out_go, 0)

    for n, (src, dst) in enumerate(pairs):
        part = src.at[0, :, :, pl.ds(0, 15 * HD)]
        pltpu.make_async_copy(part, part, in_send.at[n]).wait()
    for step, way, h in hops:
        z_copy(way, h, step).wait_send()
    for copy in (to_across, to_sibling, onward):
        copy.wait_send()

    def drain(ref, sem):
        pltpu.make_async_copy(ref, ref, sem).wait()

    @pl.when(own)
    def _():
        drain(wt.at[pl.ds(0, 240)], w_send)
        for c in range(2):
            drain(rg.at[pl.ds(0, 15), :, patches(c)], ga_send.at[c])

    @pl.when(jnp.logical_not(own))
    def _():
        drain(wt.at[pl.ds(0, 256)], w_send)
        for c in range(2):
            drain(rg.at[:, :, patches(c)], ga_send.at[c])

    for n in range(3):
        drain(so.at[n, pl.ds(0, 15)], o_send.at[n])
        drain(outs[n], o_recv.at[n])


def put(a, b, c, oa, ob, oc, sem):
    copies = [pltpu.make_async_copy(src, dst, sem.at[n]) for n, (src, dst) in enumerate(((a, oa), (b, ob), (c, oc)))]
    for copy in copies:
        copy.start()
    for copy in copies:
        copy.wait()


def body(query_saved, key_saved, value_saved, grad_block, out_weight):
    shape = jax.ShapeDtypeStruct(query_saved.shape, BF16)
    anywhere = pl.BlockSpec(memory_space=pl.ANY)
    dma = pltpu.SemaphoreType.DMA
    near = pltpu.VMEM(query_saved.shape, BF16)
    grads = pl.pallas_call(
        kernel,
        out_shape=(near, near, near),
        in_specs=[anywhere] * 5,
        out_specs=(anywhere,) * 3,
        scratch_shapes=[
            *[pltpu.VMEM((16, 4, 32, HD), BF16)] * 4,
            pltpu.VMEM((4, 4, 32, 2048), BF16),
            pltpu.VMEM((2048, 512), BF16),
            pltpu.VMEM((2, 512, 256), F32),
            pltpu.VMEM((4, 4, 4, 32, HD), BF16),
            pltpu.VMEM((2048, HD), F32),
            *[pltpu.VMEM((16, 128, HD), BF16)] * 4,
            pltpu.VMEM((16, 128, 128), F32),
            pltpu.VMEM((3, 2048, HD), F32),
            pltpu.VMEM((3, 16, 4, 32, HD), BF16),
            dma((3,)), dma((3,)),
            dma, dma,
            dma((2, 2, 4)), dma((2, 2, 4)),
            dma((4,)), dma((4,)),
            dma((2,)), dma((2,)),
            dma((3,)), dma((3,)),
        ],
        compiler_params=pltpu.CompilerParams(
            collective_id=0, has_side_effects=True, vmem_limit_bytes=60 * 1024 * 1024),
    )(query_saved, key_saved, value_saved, grad_block, out_weight.T)
    return pl.pallas_call(
        put, out_shape=(shape, shape, shape), in_specs=[pl.BlockSpec(memory_space=pltpu.VMEM)] * 3,
        out_specs=(anywhere,) * 3, scratch_shapes=[dma((3,))],
    )(*[pltpu.with_memory_space_constraint(a, pltpu.VMEM) for a in grads])


def solution(mesh):
    spec = P("dp", "seq", None, None)
    return jax.shard_map(
        body, mesh=mesh, in_specs=(spec, spec, spec, spec, P("seq", "dp")), out_specs=(spec, spec, spec), check_vma=False)
```

```python
import functools
import math

import jax
import jax.numpy as jnp
from jax import lax
from jax.experimental import pallas as pl
from jax.experimental.pallas import tpu as pltpu
from jax.sharding import PartitionSpec as P

HD = 128
F32 = jnp.float32
BF16 = jnp.bfloat16
HOP = (0, 1, 1)
MESH = pl.DeviceIdType.MESH
NT = (((1,), (1,)), ((), ()))
TN = (((0,), (0,)), ((), ()))
NN = (((1,), (0,)), ((), ()))


def dot(a, b, dims):
    return lax.dot_general(a, b, dims, preferred_element_type=F32)


def kernel(
    q, k, v, g, w, oq, ok, ov,
    rq, rk, rv, rg, gbuf, wt, ga, x32, qt, kt, vt, gt, pt, o32, so,
    in_send, in_recv, w_send, w_recv, z_send, z_recv, g_send, g_recv, ga_send, ga_recv, o_send, o_recv,
):
    dp, s = lax.axis_index("dp"), lax.axis_index("seq")
    z, u = lax.div(dp, 4), lax.rem(dp, 4)
    y, xh = lax.div(s, 2), lax.rem(s, 2)
    x, core = 2 * xh + lax.div(u, 2), lax.rem(u, 2)
    base = z * 4
    own = u == 0
    inv_root = 1.0 / math.sqrt(HD)

    def ring(i, n):
        return lax.rem(i + n, n)

    def on_x(at):
        return base + 2 * lax.rem(at, 2) + core, y * 2 + lax.div(at, 2)

    def head(j):
        return lax.rem(y + 4 * core + 2 * j + lax.div(u, 2), 8) * 2 + xh

    def holder(at):
        o = ring(y - at, 8)
        return base + 2 * lax.rem(o, 2) + lax.div(o, 4), at * 2 + xh

    up, down = ring(z + 1, 8) * 4 + u, ring(z - 1, 8) * 4 + u
    sibling = base + u + 1 - 2 * core
    right, left = on_x(ring(x + 1, 4)), on_x(ring(x - 1, 4))

    barrier = pltpu.get_barrier_semaphore()

    def greet(d, e):
        pl.semaphore_signal(barrier, inc=1, device_id=(d, e), device_id_type=MESH)

    def greet_seq(i, _):
        greet(dp, lax.rem(s + i, 16))
        return 0

    lax.fori_loop(1, 16, greet_seq, 0)

    def other(d, e):
        return jnp.logical_or(d != dp, e != s)

    def greet_group(i, _):
        d, e = holder(i)

        @pl.when(other(d, e))
        def _():
            greet(d, e)

        d, e = base + lax.rem(i, 4), head(lax.div(i, 4))

        @pl.when(other(d, e))
        def _():
            greet(d, e)

        return 0

    lax.fori_loop(0, 8, greet_group, 0)
    for d, e in ((up, s), (down, s), (sibling, s), left, right):
        greet(d, e)
    pl.semaphore_wait(barrier, 36 - 2 * own.astype(jnp.int32))

    def w_rows(at):
        j = lax.rem(lax.div(ring(y - at, 8), 2), 2)
        return wt.at[pl.ds(pl.multiple_of(dp * 64, 64), 64), pl.ds(pl.multiple_of(j * HD, HD), HD)]

    def w_go(i, _):
        at = lax.rem(y + i, 8)
        d, e = holder(at)

        @pl.when(other(d, e))
        def _():
            pltpu.make_async_remote_copy(
                src_ref=w, dst_ref=w_rows(at), send_sem=w_send, recv_sem=w_recv,
                device_id=(d, e), device_id_type=MESH).start()

        @pl.when(jnp.logical_not(other(d, e)))
        def _():
            pltpu.make_async_copy(w, w_rows(at), w_recv).start()

        return 0

    lax.fori_loop(0, 8, w_go, 0)

    def block(at, c):
        return gbuf.at[2 * at + c]

    def g_copy(n, src, dst, to):
        return pltpu.make_async_remote_copy(
            src_ref=src, dst_ref=dst, send_sem=g_send.at[n], recv_sem=g_recv.at[n],
            device_id=to, device_id_type=MESH)

    twin = (sibling, s)
    mine, before, after, across = (block(ring(x + i, 4), core) for i in (0, -1, 1, 2))
    near, far = pl.ds(0, 2), pl.ds(2, 2)
    g_own = pltpu.make_async_copy(g.at[0], mine, g_recv.at[0])
    to_right = g_copy(1, g.at[0], mine, right)
    to_left = g_copy(2, g.at[0], mine, left)
    to_twin = g_copy(3, g.at[0], mine, twin)
    on_right = g_copy(4, before.at[near], before.at[near], right)
    on_left = g_copy(5, after.at[far], after.at[far], left)
    twin_before = g_copy(6, before, before, twin)
    twin_after = g_copy(7, after, after, twin)
    twin_near = g_copy(8, across.at[near], across.at[near], twin)
    twin_far = g_copy(9, across.at[far], across.at[far], twin)
    for copy in (g_own, to_right, to_left, to_twin):
        copy.start()

    pairs = ((q, rq), (k, rk), (v, rv))

    def lanes(h):
        return pl.ds(pl.multiple_of(h * HD, HD), HD)

    def send_in(flip):
        for n, (src, dst) in enumerate(pairs):

            def in_go(i, _, src=src, dst=dst, n=n):
                t = lax.rem(y + i, 8) * 2 + (1 - xh if flip else xh)
                pltpu.make_async_remote_copy(
                    src_ref=src.at[0, :, :, lanes(t)], dst_ref=dst.at[s], send_sem=in_send.at[n], recv_sem=in_recv.at[n],
                    device_id=(dp, t), device_id_type=MESH).start()
                return 0

            lax.fori_loop(0 if flip else 1, 8, in_go, 0)

    for n, (src, dst) in enumerate(pairs):
        pltpu.make_async_copy(src.at[0, :, :, lanes(s)], dst.at[s], in_recv.at[n]).start()
    send_in(False)

    def z_copy(way, h, step):
        slab = ring(z - step, 8) if way == 0 else ring(z + step, 8)
        rows = wt.at[pl.ds(pl.multiple_of(slab * 256 + h * 128, 128), 128)]
        return pltpu.make_async_remote_copy(
            src_ref=rows, dst_ref=rows, send_sem=z_send.at[way, h, step], recv_sem=z_recv.at[way, h, step],
            device_id=(up if way == 0 else down, s), device_id_type=MESH)

    def z_arrived(way, h, step):
        slab = ring(z - step - 1, 8) if way == 0 else ring(z + step + 1, 8)
        rows = wt.at[pl.ds(pl.multiple_of(slab * 256 + h * 128, 128), 128)]
        pltpu.make_async_remote_copy(
            src_ref=rows, dst_ref=rows, send_sem=z_send.at[way, h, step], recv_sem=z_recv.at[way, h, step],
            device_id=(up if way == 0 else down, s), device_id_type=MESH).wait_recv()

    hops = [(step, way, h) for step in range(4) for h in range(2) for way in range(2) if step < 3 or way == h]
    slab = wt.at[pl.ds(pl.multiple_of(z * 256, 256), 256)]
    pltpu.make_async_copy(slab, slab, w_recv).wait()

    def first_hop():
        to_right.wait_recv()
        on_right.start()
        twin_before.start()
        to_left.wait_recv()
        on_left.start()
        twin_after.start()
        send_in(True)

    for step, way, h in hops:
        if step:
            z_arrived(way, h, step - 1)
        z_copy(way, h, step).start()
        if (step, way, h) == HOP:
            first_hop()
    on_right.wait_recv()
    twin_near.start()
    on_left.wait_recv()
    twin_far.start()
    for way, h in ((0, 1), (1, 0)):
        z_arrived(way, h, 2)
    for way in range(2):
        z_arrived(way, way, 3)
    g_own.wait()
    for copy in (to_twin, twin_before, twin_after, twin_near, twin_far):
        copy.wait_recv()

    for half in range(2):
        val = dot(gbuf[4 * half : 4 * half + 4].reshape(512, 2048), wt[...], NN).astype(BF16)
        for j in range(2):
            ga[j, 4 * half : 4 * half + 4] = val[:, j * HD : (j + 1) * HD].reshape(4, 4, 32, HD)

    def patches(c):
        return pl.ds(c * 16, 16)

    for c in range(2):

        def ga_go(i, _, c=c):
            t = lax.rem(s + i, 16)
            b, j = lax.rem(t, 8), lax.div(t, 8)
            at = lax.div(b, 2)
            d, e = base + 2 * lax.rem(at, 2) + lax.rem(b, 2), head(j)
            src, dst = ga.at[j, b, :, patches(c)], rg.at[2 * y + lax.div(at, 2), :, patches(c)]

            @pl.when(other(d, e))
            def _():
                pltpu.make_async_remote_copy(
                    src_ref=src, dst_ref=dst, send_sem=ga_send.at[c], recv_sem=ga_recv.at[c],
                    device_id=(d, e), device_id_type=MESH).start()

            @pl.when(jnp.logical_not(other(d, e)))
            def _():
                pltpu.make_async_copy(src, dst, ga_recv.at[c]).start()

            return 0

        lax.fori_loop(0, 16, ga_go, 0)

    key_at = lax.broadcasted_iota(jnp.int32, (128, 128), 0)
    query_at = lax.broadcasted_iota(jnp.int32, (128, 128), 1)
    seen = jnp.logical_and(query_at >= key_at, (query_at >= 64) == (key_at >= 64))

    def widen(src):
        def step(i, _):
            x32[pl.ds(pl.multiple_of(i * 128, 128), 128)] = src[i].reshape(128, HD).astype(F32)
            return 0

        lax.fori_loop(0, 16, step, 0)

    def pair_of(p):
        a = x32[pl.ds(2 * p, 64, stride=32), :]
        b = x32[pl.ds(2 * p + 1, 64, stride=32), :]
        return jnp.concatenate([a, b], axis=0).astype(BF16)

    for n, (dst, out) in enumerate(((rq, qt), (rk, kt), (rv, vt))):
        pltpu.make_async_copy(dst, dst, in_recv.at[n]).wait()
        widen(dst)

        def regroup(p, _, out=out):
            out[p] = pair_of(p)
            return 0

        lax.fori_loop(0, 16, regroup, 0)

    def soft(p, _):
        scores = jnp.where(seen, dot(kt[p], qt[p], NT) * inv_root, -1e30)
        e = jnp.exp(scores - jnp.max(scores, axis=0, keepdims=True))
        pt[p] = e / jnp.sum(e, axis=0, keepdims=True)
        return 0

    lax.fori_loop(0, 16, soft, 0)

    outs = (oq, ok, ov)

    def out_copy(n, c, d):
        return pltpu.make_async_remote_copy(
            src_ref=so.at[n, d, :, patches(c)], dst_ref=outs[n].at[0, :, patches(c), lanes(s)],
            send_sem=o_send.at[n], recv_sem=o_recv.at[n],
            device_id=(dp, d), device_id_type=MESH)

    for c in range(2):
        part = rg.at[:, :, patches(c)]
        pltpu.make_async_copy(part, part, ga_recv.at[c]).wait()

        def widen_g(i, _, c=c):
            for f in range(4):
                x32[pl.ds(pl.multiple_of(i * 128 + f * 32 + c * 16, 16), 16)] = rg[i, f, c * 16 : c * 16 + 16].astype(F32)
            return 0

        lax.fori_loop(0, 16, widen_g, 0)

        def grads(p, _):
            gp, vp, prob = pair_of(p), vt[p], pt[p]
            low = prob.astype(BF16)
            grad_prob = dot(vp, gp, NT)
            delta = jnp.sum(low.astype(F32) * grad_prob, axis=0, keepdims=True)
            ds = (prob * (grad_prob - delta) * inv_root).astype(BF16)
            for n, val in ((2, dot(low, gp, NN)), (1, dot(ds, qt[p], NN)), (0, dot(ds, kt[p], TN))):
                o32[n, pl.ds(2 * p, 64, stride=32), :] = val[:64]
                o32[n, pl.ds(2 * p + 1, 64, stride=32), :] = val[64:]
            return 0

        lax.fori_loop(c * 8, c * 8 + 8, grads, 0)

        for n in range(3):

            def narrow(i, _, n=n, c=c):
                for f in range(4):
                    rows = pl.ds(pl.multiple_of(i * 128 + f * 32 + c * 16, 16), 16)
                    so[n, i, f, c * 16 : c * 16 + 16] = o32[n, rows, :].astype(BF16)
                return 0

            lax.fori_loop(0, 16, narrow, 0)
            pltpu.make_async_copy(
                so.at[n, s, :, patches(c)], outs[n].at[0, :, patches(c), lanes(s)], o_recv.at[n]).start()

            def out_go(i, _, n=n, c=c):
                out_copy(n, c, lax.rem(s + i, 16)).start()
                return 0

            lax.fori_loop(1, 16, out_go, 0)

    for n, (src, dst) in enumerate(pairs):
        part = src.at[0, :, :, pl.ds(0, 15 * HD)]
        pltpu.make_async_copy(part, part, in_send.at[n]).wait()
    for step, way, h in hops:
        z_copy(way, h, step).wait_send()
    for copy in (to_right, to_left, to_twin, on_right, on_left, twin_before, twin_after, twin_near, twin_far):
        copy.wait_send()

    def drain(ref, sem):
        pltpu.make_async_copy(ref, ref, sem).wait()

    @pl.when(own)
    def _():
        drain(wt.at[pl.ds(0, 224)], w_send)
        for c in range(2):
            drain(rg.at[pl.ds(0, 14), :, patches(c)], ga_send.at[c])

    @pl.when(jnp.logical_not(own))
    def _():
        drain(wt.at[pl.ds(0, 256)], w_send)
        for c in range(2):
            drain(rg.at[:, :, patches(c)], ga_send.at[c])

    for n in range(3):
        drain(so.at[n, pl.ds(0, 15)], o_send.at[n])
        drain(outs[n], o_recv.at[n])


def put(a, b, c, oa, ob, oc, sem):
    copies = [pltpu.make_async_copy(src, dst, sem.at[n]) for n, (src, dst) in enumerate(((a, oa), (b, ob), (c, oc)))]
    for copy in copies:
        copy.start()
    for copy in copies:
        copy.wait()


def body(query_saved, key_saved, value_saved, grad_block, out_weight):
    shape = jax.ShapeDtypeStruct(query_saved.shape, BF16)
    anywhere = pl.BlockSpec(memory_space=pl.ANY)
    dma = pltpu.SemaphoreType.DMA
    near = pltpu.VMEM(query_saved.shape, BF16)
    grads = pl.pallas_call(
        kernel,
        out_shape=(near, near, near),
        in_specs=[anywhere] * 5,
        out_specs=(anywhere,) * 3,
        scratch_shapes=[
            *[pltpu.VMEM((16, 4, 32, HD), BF16)] * 4,
            pltpu.VMEM((8, 4, 32, 2048), BF16),
            pltpu.VMEM((2048, 256), BF16),
            pltpu.VMEM((2, 8, 4, 32, HD), BF16),
            pltpu.VMEM((2048, HD), F32),
            *[pltpu.VMEM((16, 128, HD), BF16)] * 4,
            pltpu.VMEM((16, 128, 128), F32),
            pltpu.VMEM((3, 2048, HD), F32),
            pltpu.VMEM((3, 16, 4, 32, HD), BF16),
            dma((3,)), dma((3,)),
            dma, dma,
            dma((2, 2, 4)), dma((2, 2, 4)),
            dma((10,)), dma((10,)),
            dma((2,)), dma((2,)),
            dma((3,)), dma((3,)),
        ],
        compiler_params=pltpu.CompilerParams(
            collective_id=0, has_side_effects=True, vmem_limit_bytes=60 * 1024 * 1024),
    )(query_saved, key_saved, value_saved, grad_block, out_weight.T)
    return pl.pallas_call(
        put, out_shape=(shape, shape, shape), in_specs=[pl.BlockSpec(memory_space=pltpu.VMEM)] * 3,
        out_specs=(anywhere,) * 3, scratch_shapes=[dma((3,))],
    )(*[pltpu.with_memory_space_constraint(a, pltpu.VMEM) for a in grads])


def solution(mesh):
    spec = P("dp", "seq", None, None)
    return jax.shard_map(
        body, mesh=mesh, in_specs=(spec, spec, spec, spec, P("seq", "dp")), out_specs=(spec, spec, spec), check_vma=False)
```

```python
import functools
import math

import jax
import jax.numpy as jnp
from jax import lax
from jax.experimental import pallas as pl
from jax.experimental.pallas import tpu as pltpu
from jax.sharding import PartitionSpec as P

HD = 128
F32 = jnp.float32
BF16 = jnp.bfloat16
HOP = (0, 1, 1)
MESH = pl.DeviceIdType.MESH
NT = (((1,), (1,)), ((), ()))
TN = (((0,), (0,)), ((), ()))
NN = (((1,), (0,)), ((), ()))


def dot(a, b, dims):
    return lax.dot_general(a, b, dims, preferred_element_type=F32)


def kernel(
    q, k, v, g, w, oq, ok, ov,
    rq, rk, rv, rg, gbuf, wt, ga, x32, qt, kt, vt, gt, pt, o32, so,
    in_send, in_recv, w_send, w_recv, z_send, z_recv, g_send, g_recv, ga_send, ga_recv, o_send, o_recv,
):
    dp, s = lax.axis_index("dp"), lax.axis_index("seq")
    z, u = lax.div(dp, 4), lax.rem(dp, 4)
    y, xh = lax.div(s, 2), lax.rem(s, 2)
    x, core = 2 * xh + lax.div(u, 2), lax.rem(u, 2)
    base = z * 4
    own = u == 0
    inv_root = 1.0 / math.sqrt(HD)

    def ring(i, n):
        return lax.rem(i + n, n)

    def on_x(at):
        return base + 2 * lax.rem(at, 2) + core, y * 2 + lax.div(at, 2)

    def head(j):
        return lax.rem(y + 4 * core + 2 * j + lax.div(u, 2), 8) * 2 + xh

    def holder(at):
        o = ring(y - at, 8)
        return base + 2 * lax.rem(o, 2) + lax.div(o, 4), at * 2 + xh

    up, down = ring(z + 1, 8) * 4 + u, ring(z - 1, 8) * 4 + u
    sibling = base + u + 1 - 2 * core
    right, left = on_x(ring(x + 1, 4)), on_x(ring(x - 1, 4))

    barrier = pltpu.get_barrier_semaphore()

    def greet(d, e):
        pl.semaphore_signal(barrier, inc=1, device_id=(d, e), device_id_type=MESH)

    def greet_seq(i, _):
        greet(dp, lax.rem(s + i, 16))
        return 0

    lax.fori_loop(1, 16, greet_seq, 0)

    def other(d, e):
        return jnp.logical_or(d != dp, e != s)

    def greet_group(i, _):
        d, e = holder(i)

        @pl.when(other(d, e))
        def _():
            greet(d, e)

        d, e = base + lax.rem(i, 4), head(lax.div(i, 4))

        @pl.when(other(d, e))
        def _():
            greet(d, e)

        return 0

    lax.fori_loop(0, 8, greet_group, 0)
    for d, e in ((up, s), (down, s), (sibling, s), left, right):
        greet(d, e)
    pl.semaphore_wait(barrier, 36 - 2 * own.astype(jnp.int32))

    def w_rows(at):
        j = lax.rem(lax.div(ring(y - at, 8), 2), 2)
        return wt.at[pl.ds(pl.multiple_of(dp * 64, 64), 64), pl.ds(pl.multiple_of(j * HD, HD), HD)]

    def w_go(i, _):
        at = lax.rem(y + i, 8)
        d, e = holder(at)

        @pl.when(other(d, e))
        def _():
            pltpu.make_async_remote_copy(
                src_ref=w, dst_ref=w_rows(at), send_sem=w_send, recv_sem=w_recv,
                device_id=(d, e), device_id_type=MESH).start()

        @pl.when(jnp.logical_not(other(d, e)))
        def _():
            pltpu.make_async_copy(w, w_rows(at), w_recv).start()

        return 0

    lax.fori_loop(0, 8, w_go, 0)

    def block(at, c):
        return gbuf.at[2 * at + c]

    def g_copy(n, src, dst, to):
        return pltpu.make_async_remote_copy(
            src_ref=src, dst_ref=dst, send_sem=g_send.at[n], recv_sem=g_recv.at[n],
            device_id=to, device_id_type=MESH)

    twin = (sibling, s)
    mine, before, after, across = (block(ring(x + i, 4), core) for i in (0, -1, 1, 2))
    near, far = pl.ds(0, 2), pl.ds(2, 2)
    g_own = pltpu.make_async_copy(g.at[0], mine, g_recv.at[0])
    to_right = g_copy(1, g.at[0], mine, right)
    to_left = g_copy(2, g.at[0], mine, left)
    to_twin = g_copy(3, g.at[0], mine, twin)
    on_right = g_copy(4, before.at[near], before.at[near], right)
    on_left = g_copy(5, after.at[far], after.at[far], left)
    twin_before = g_copy(6, before, before, twin)
    twin_after = g_copy(7, after, after, twin)
    twin_near = g_copy(8, across.at[near], across.at[near], twin)
    twin_far = g_copy(9, across.at[far], across.at[far], twin)
    for copy in (g_own, to_right, to_left, to_twin):
        copy.start()

    pairs = ((q, rq), (k, rk), (v, rv))

    def lanes(h):
        return pl.ds(pl.multiple_of(h * HD, HD), HD)

    def send_in(flip):
        for n, (src, dst) in enumerate(pairs):

            def in_go(i, _, src=src, dst=dst, n=n):
                t = lax.rem(y + i, 8) * 2 + (1 - xh if flip else xh)
                pltpu.make_async_remote_copy(
                    src_ref=src.at[0, :, :, lanes(t)], dst_ref=dst.at[s], send_sem=in_send.at[n], recv_sem=in_recv.at[n],
                    device_id=(dp, t), device_id_type=MESH).start()
                return 0

            lax.fori_loop(0 if flip else 1, 8, in_go, 0)

    for n, (src, dst) in enumerate(pairs):
        pltpu.make_async_copy(src.at[0, :, :, lanes(s)], dst.at[s], in_recv.at[n]).start()
    send_in(False)

    def z_copy(way, h, step):
        slab = ring(z - step, 8) if way == 0 else ring(z + step, 8)
        rows = wt.at[pl.ds(pl.multiple_of(slab * 256 + h * 128, 128), 128)]
        return pltpu.make_async_remote_copy(
            src_ref=rows, dst_ref=rows, send_sem=z_send.at[way, h, step], recv_sem=z_recv.at[way, h, step],
            device_id=(up if way == 0 else down, s), device_id_type=MESH)

    def z_arrived(way, h, step):
        slab = ring(z - step - 1, 8) if way == 0 else ring(z + step + 1, 8)
        rows = wt.at[pl.ds(pl.multiple_of(slab * 256 + h * 128, 128), 128)]
        pltpu.make_async_remote_copy(
            src_ref=rows, dst_ref=rows, send_sem=z_send.at[way, h, step], recv_sem=z_recv.at[way, h, step],
            device_id=(up if way == 0 else down, s), device_id_type=MESH).wait_recv()

    hops = [(step, way, h) for step in range(4) for h in range(2) for way in range(2) if step < 3 or way == h]
    slab = wt.at[pl.ds(pl.multiple_of(z * 256, 256), 256)]
    pltpu.make_async_copy(slab, slab, w_recv).wait()

    def first_hop():
        to_right.wait_recv()
        on_right.start()
        twin_before.start()
        to_left.wait_recv()
        on_left.start()
        twin_after.start()
        send_in(True)

    for step, way, h in hops:
        if step:
            z_arrived(way, h, step - 1)
        z_copy(way, h, step).start()
        if (step, way, h) == HOP:
            first_hop()
    on_right.wait_recv()
    twin_near.start()
    on_left.wait_recv()
    twin_far.start()
    for way, h in ((0, 1), (1, 0)):
        z_arrived(way, h, 2)
    for way in range(2):
        z_arrived(way, way, 3)
    g_own.wait()
    for copy in (to_twin, twin_before, twin_after, twin_near, twin_far):
        copy.wait_recv()

    for half in range(2):
        val = dot(gbuf[4 * half : 4 * half + 4].reshape(512, 2048), wt[...], NN).astype(BF16)
        for j in range(2):
            ga[j, 4 * half : 4 * half + 4] = val[:, j * HD : (j + 1) * HD].reshape(4, 4, 32, HD)

    def patches(c):
        return pl.ds(c * 16, 16)

    for c in range(2):

        def ga_go(i, _, c=c):
            t = lax.rem(s + i, 16)
            b, j = lax.rem(t, 8), lax.div(t, 8)
            at = lax.div(b, 2)
            d, e = base + 2 * lax.rem(at, 2) + lax.rem(b, 2), head(j)
            src, dst = ga.at[j, b, :, patches(c)], rg.at[2 * y + lax.div(at, 2), :, patches(c)]

            @pl.when(other(d, e))
            def _():
                pltpu.make_async_remote_copy(
                    src_ref=src, dst_ref=dst, send_sem=ga_send.at[c], recv_sem=ga_recv.at[c],
                    device_id=(d, e), device_id_type=MESH).start()

            @pl.when(jnp.logical_not(other(d, e)))
            def _():
                pltpu.make_async_copy(src, dst, ga_recv.at[c]).start()

            return 0

        lax.fori_loop(0, 16, ga_go, 0)

    key_at = lax.broadcasted_iota(jnp.int32, (128, 128), 0)
    query_at = lax.broadcasted_iota(jnp.int32, (128, 128), 1)
    seen = jnp.logical_and(query_at >= key_at, (query_at >= 64) == (key_at >= 64))

    def widen(src):
        def step(i, _):
            x32[pl.ds(pl.multiple_of(i * 128, 128), 128)] = src[i].reshape(128, HD).astype(F32)
            return 0

        lax.fori_loop(0, 16, step, 0)

    def pair_of(p):
        a = x32[pl.ds(2 * p, 64, stride=32), :]
        b = x32[pl.ds(2 * p + 1, 64, stride=32), :]
        return jnp.concatenate([a, b], axis=0).astype(BF16)

    for n, (dst, out) in enumerate(((rq, qt), (rk, kt), (rv, vt))):
        pltpu.make_async_copy(dst, dst, in_recv.at[n]).wait()
        widen(dst)

        def regroup(p, _, out=out):
            out[p] = pair_of(p)
            return 0

        lax.fori_loop(0, 16, regroup, 0)

    def soft(p, _):
        scores = jnp.where(seen, dot(kt[p], qt[p], NT) * inv_root, -1e30)
        e = jnp.exp(scores - jnp.max(scores, axis=0, keepdims=True))
        pt[p] = e / jnp.sum(e, axis=0, keepdims=True)
        return 0

    lax.fori_loop(0, 16, soft, 0)

    outs = (oq, ok, ov)

    def out_copy(n, c, d):
        return pltpu.make_async_remote_copy(
            src_ref=so.at[n, d, :, patches(c)], dst_ref=outs[n].at[0, :, patches(c), lanes(s)],
            send_sem=o_send.at[n], recv_sem=o_recv.at[n],
            device_id=(dp, d), device_id_type=MESH)

    for c in range(2):
        part = rg.at[:, :, patches(c)]
        pltpu.make_async_copy(part, part, ga_recv.at[c]).wait()

        def widen_g(i, _, c=c):
            for f in range(4):
                x32[pl.ds(pl.multiple_of(i * 128 + f * 32 + c * 16, 16), 16)] = rg[i, f, c * 16 : c * 16 + 16].astype(F32)
            return 0

        lax.fori_loop(0, 16, widen_g, 0)

        def value_grad(p, _):
            gp = pair_of(p)
            gt[p] = gp
            val = dot(pt[p].astype(BF16), gp, NN)
            o32[2, pl.ds(2 * p, 64, stride=32), :] = val[:64]
            o32[2, pl.ds(2 * p + 1, 64, stride=32), :] = val[64:]
            return 0

        def score_grads(p, _):
            prob = pt[p]
            grad_prob = dot(vt[p], gt[p], NT)
            delta = jnp.sum(prob.astype(BF16).astype(F32) * grad_prob, axis=0, keepdims=True)
            ds = (prob * (grad_prob - delta) * inv_root).astype(BF16)
            for n, val in ((1, dot(ds, qt[p], NN)), (0, dot(ds, kt[p], TN))):
                o32[n, pl.ds(2 * p, 64, stride=32), :] = val[:64]
                o32[n, pl.ds(2 * p + 1, 64, stride=32), :] = val[64:]
            return 0

        def give(n, c=c):
            def narrow(i, _):
                for f in range(4):
                    rows = pl.ds(pl.multiple_of(i * 128 + f * 32 + c * 16, 16), 16)
                    so[n, i, f, c * 16 : c * 16 + 16] = o32[n, rows, :].astype(BF16)
                return 0

            lax.fori_loop(0, 16, narrow, 0)
            pltpu.make_async_copy(
                so.at[n, s, :, patches(c)], outs[n].at[0, :, patches(c), lanes(s)], o_recv.at[n]).start()

            def out_go(i, _):
                out_copy(n, c, lax.rem(s + i, 16)).start()
                return 0

            lax.fori_loop(1, 16, out_go, 0)

        lax.fori_loop(c * 8, c * 8 + 8, value_grad, 0)
        give(2)
        lax.fori_loop(c * 8, c * 8 + 8, score_grads, 0)
        give(1)
        give(0)

    for n, (src, dst) in enumerate(pairs):
        part = src.at[0, :, :, pl.ds(0, 15 * HD)]
        pltpu.make_async_copy(part, part, in_send.at[n]).wait()
    for step, way, h in hops:
        z_copy(way, h, step).wait_send()
    for copy in (to_right, to_left, to_twin, on_right, on_left, twin_before, twin_after, twin_near, twin_far):
        copy.wait_send()

    def drain(ref, sem):
        pltpu.make_async_copy(ref, ref, sem).wait()

    @pl.when(own)
    def _():
        drain(wt.at[pl.ds(0, 224)], w_send)
        for c in range(2):
            drain(rg.at[pl.ds(0, 14), :, patches(c)], ga_send.at[c])

    @pl.when(jnp.logical_not(own))
    def _():
        drain(wt.at[pl.ds(0, 256)], w_send)
        for c in range(2):
            drain(rg.at[:, :, patches(c)], ga_send.at[c])

    for n in range(3):
        drain(so.at[n, pl.ds(0, 15)], o_send.at[n])
        drain(outs[n], o_recv.at[n])


def put(a, b, c, oa, ob, oc, sem):
    copies = [pltpu.make_async_copy(src, dst, sem.at[n]) for n, (src, dst) in enumerate(((a, oa), (b, ob), (c, oc)))]
    for copy in copies:
        copy.start()
    for copy in copies:
        copy.wait()


def body(query_saved, key_saved, value_saved, grad_block, out_weight):
    shape = jax.ShapeDtypeStruct(query_saved.shape, BF16)
    anywhere = pl.BlockSpec(memory_space=pl.ANY)
    dma = pltpu.SemaphoreType.DMA
    near = pltpu.VMEM(query_saved.shape, BF16)
    grads = pl.pallas_call(
        kernel,
        out_shape=(near, near, near),
        in_specs=[anywhere] * 5,
        out_specs=(anywhere,) * 3,
        scratch_shapes=[
            *[pltpu.VMEM((16, 4, 32, HD), BF16)] * 4,
            pltpu.VMEM((8, 4, 32, 2048), BF16),
            pltpu.VMEM((2048, 256), BF16),
            pltpu.VMEM((2, 8, 4, 32, HD), BF16),
            pltpu.VMEM((2048, HD), F32),
            *[pltpu.VMEM((16, 128, HD), BF16)] * 4,
            pltpu.VMEM((16, 128, 128), F32),
            pltpu.VMEM((3, 2048, HD), F32),
            pltpu.VMEM((3, 16, 4, 32, HD), BF16),
            dma((3,)), dma((3,)),
            dma, dma,
            dma((2, 2, 4)), dma((2, 2, 4)),
            dma((10,)), dma((10,)),
            dma((2,)), dma((2,)),
            dma((3,)), dma((3,)),
        ],
        compiler_params=pltpu.CompilerParams(
            collective_id=0, has_side_effects=True, vmem_limit_bytes=60 * 1024 * 1024),
    )(query_saved, key_saved, value_saved, grad_block, out_weight.T)
    return pl.pallas_call(
        put, out_shape=(shape, shape, shape), in_specs=[pl.BlockSpec(memory_space=pltpu.VMEM)] * 3,
        out_specs=(anywhere,) * 3, scratch_shapes=[dma((3,))],
    )(*[pltpu.with_memory_space_constraint(a, pltpu.VMEM) for a in grads])


def solution(mesh):
    spec = P("dp", "seq", None, None)
    return jax.shard_map(
        body, mesh=mesh, in_specs=(spec, spec, spec, spec, P("seq", "dp")), out_specs=(spec, spec, spec), check_vma=False)
```

```python
import functools
import math

import jax
import jax.numpy as jnp
from jax import lax
from jax.experimental import pallas as pl
from jax.experimental.pallas import tpu as pltpu
from jax.sharding import PartitionSpec as P

HD = 128
F32 = jnp.float32
BF16 = jnp.bfloat16
HOP = (0, 1, 1)
MESH = pl.DeviceIdType.MESH
NT = (((1,), (1,)), ((), ()))
TN = (((0,), (0,)), ((), ()))
NN = (((1,), (0,)), ((), ()))


def dot(a, b, dims):
    return lax.dot_general(a, b, dims, preferred_element_type=F32)


def kernel(
    q, k, v, g, w, oq, ok, ov,
    rq, rk, rv, rg, gbuf, wt, ga, x32, qt, kt, vt, gt, pt, o32, so,
    in_send, in_recv, w_send, w_recv, z_send, z_recv, g_send, g_recv, ga_send, ga_recv, o_send, o_recv,
):
    dp, s = lax.axis_index("dp"), lax.axis_index("seq")
    z, u = lax.div(dp, 4), lax.rem(dp, 4)
    y, xh = lax.div(s, 2), lax.rem(s, 2)
    x, core = 2 * xh + lax.div(u, 2), lax.rem(u, 2)
    base = z * 4
    own = u == 0
    inv_root = 1.0 / math.sqrt(HD)

    def ring(i, n):
        return lax.rem(i + n, n)

    def on_x(at):
        return base + 2 * lax.rem(at, 2) + core, y * 2 + lax.div(at, 2)

    def head(j):
        return lax.rem(y + 4 * core + 2 * j + lax.div(u, 2), 8) * 2 + xh

    def holder(at):
        o = ring(y - at, 8)
        return base + 2 * lax.rem(o, 2) + lax.div(o, 4), at * 2 + xh

    up, down = ring(z + 1, 8) * 4 + u, ring(z - 1, 8) * 4 + u
    sibling = base + u + 1 - 2 * core
    right, left = on_x(ring(x + 1, 4)), on_x(ring(x - 1, 4))

    barrier = pltpu.get_barrier_semaphore()

    def greet(d, e):
        pl.semaphore_signal(barrier, inc=1, device_id=(d, e), device_id_type=MESH)

    def greet_seq(i, _):
        greet(dp, lax.rem(s + i, 16))
        return 0

    lax.fori_loop(1, 16, greet_seq, 0)

    def other(d, e):
        return jnp.logical_or(d != dp, e != s)

    def greet_group(i, _):
        d, e = holder(i)

        @pl.when(other(d, e))
        def _():
            greet(d, e)

        d, e = base + lax.rem(i, 4), head(lax.div(i, 4))

        @pl.when(other(d, e))
        def _():
            greet(d, e)

        return 0

    lax.fori_loop(0, 8, greet_group, 0)
    for d, e in ((up, s), (down, s), (sibling, s), left, right):
        greet(d, e)
    pl.semaphore_wait(barrier, 36 - 2 * own.astype(jnp.int32))

    def w_rows(at):
        j = lax.rem(lax.div(ring(y - at, 8), 2), 2)
        return wt.at[pl.ds(pl.multiple_of(dp * 64, 64), 64), pl.ds(pl.multiple_of(j * HD, HD), HD)]

    def w_go(i, _):
        at = lax.rem(y + i, 8)
        d, e = holder(at)

        @pl.when(other(d, e))
        def _():
            pltpu.make_async_remote_copy(
                src_ref=w, dst_ref=w_rows(at), send_sem=w_send, recv_sem=w_recv,
                device_id=(d, e), device_id_type=MESH).start()

        @pl.when(jnp.logical_not(other(d, e)))
        def _():
            pltpu.make_async_copy(w, w_rows(at), w_recv).start()

        return 0

    lax.fori_loop(0, 8, w_go, 0)

    def block(at, c):
        return gbuf.at[2 * at + c]

    def g_copy(n, src, dst, to):
        return pltpu.make_async_remote_copy(
            src_ref=src, dst_ref=dst, send_sem=g_send.at[n], recv_sem=g_recv.at[n],
            device_id=to, device_id_type=MESH)

    twin = (sibling, s)
    mine, before, after, across = (block(ring(x + i, 4), core) for i in (0, -1, 1, 2))
    near, far = pl.ds(0, 2), pl.ds(2, 2)
    g_own = pltpu.make_async_copy(g.at[0], mine, g_recv.at[0])
    to_right = g_copy(1, g.at[0], mine, right)
    to_left = g_copy(2, g.at[0], mine, left)
    to_twin = g_copy(3, g.at[0], mine, twin)
    on_right = g_copy(4, before.at[near], before.at[near], right)
    on_left = g_copy(5, after.at[far], after.at[far], left)
    twin_before = g_copy(6, before, before, twin)
    twin_after = g_copy(7, after, after, twin)
    twin_near = g_copy(8, across.at[near], across.at[near], twin)
    twin_far = g_copy(9, across.at[far], across.at[far], twin)
    for copy in (g_own, to_right, to_left, to_twin):
        copy.start()

    pairs = ((q, rq), (k, rk), (v, rv))

    def lanes(h):
        return pl.ds(pl.multiple_of(h * HD, HD), HD)

    def send_in(flip):
        for n, (src, dst) in enumerate(pairs):

            def in_go(i, _, src=src, dst=dst, n=n):
                t = lax.rem(y + i, 8) * 2 + (1 - xh if flip else xh)
                pltpu.make_async_remote_copy(
                    src_ref=src.at[0, :, :, lanes(t)], dst_ref=dst.at[s], send_sem=in_send.at[n], recv_sem=in_recv.at[n],
                    device_id=(dp, t), device_id_type=MESH).start()
                return 0

            lax.fori_loop(0 if flip else 1, 8, in_go, 0)

    for n, (src, dst) in enumerate(pairs):
        pltpu.make_async_copy(src.at[0, :, :, lanes(s)], dst.at[s], in_recv.at[n]).start()
    send_in(False)

    def z_copy(way, h, step):
        slab = ring(z - step, 8) if way == 0 else ring(z + step, 8)
        rows = wt.at[pl.ds(pl.multiple_of(slab * 256 + h * 128, 128), 128)]
        return pltpu.make_async_remote_copy(
            src_ref=rows, dst_ref=rows, send_sem=z_send.at[way, h, step], recv_sem=z_recv.at[way, h, step],
            device_id=(up if way == 0 else down, s), device_id_type=MESH)

    def z_arrived(way, h, step):
        slab = ring(z - step - 1, 8) if way == 0 else ring(z + step + 1, 8)
        rows = wt.at[pl.ds(pl.multiple_of(slab * 256 + h * 128, 128), 128)]
        pltpu.make_async_remote_copy(
            src_ref=rows, dst_ref=rows, send_sem=z_send.at[way, h, step], recv_sem=z_recv.at[way, h, step],
            device_id=(up if way == 0 else down, s), device_id_type=MESH).wait_recv()

    hops = [(step, way, h) for step in range(4) for h in range(2) for way in range(2) if step < 3 or way == h]
    slab = wt.at[pl.ds(pl.multiple_of(z * 256, 256), 256)]
    pltpu.make_async_copy(slab, slab, w_recv).wait()

    def first_hop():
        to_right.wait_recv()
        on_right.start()
        twin_before.start()
        to_left.wait_recv()
        on_left.start()
        twin_after.start()
        send_in(True)

    for step, way, h in hops:
        if step:
            z_arrived(way, h, step - 1)
        z_copy(way, h, step).start()
        if (step, way, h) == HOP:
            first_hop()
    on_right.wait_recv()
    twin_near.start()
    on_left.wait_recv()
    twin_far.start()
    for way, h in ((0, 1), (1, 0)):
        z_arrived(way, h, 2)
    for way in range(2):
        z_arrived(way, way, 3)
    g_own.wait()
    for copy in (to_twin, twin_before, twin_after, twin_near, twin_far):
        copy.wait_recv()

    for half in range(2):
        val = dot(gbuf[4 * half : 4 * half + 4].reshape(512, 2048), wt[...], NN).astype(BF16)
        for j in range(2):
            ga[j, 4 * half : 4 * half + 4] = val[:, j * HD : (j + 1) * HD].reshape(4, 4, 32, HD)

    def patches(c):
        return pl.ds(c * 16, 16)

    for c in range(2):

        def ga_go(i, _, c=c):
            t = lax.rem(s + i, 16)
            b, j = lax.rem(t, 8), lax.div(t, 8)
            at = lax.div(b, 2)
            d, e = base + 2 * lax.rem(at, 2) + lax.rem(b, 2), head(j)
            src, dst = ga.at[j, b, :, patches(c)], rg.at[2 * y + lax.div(at, 2), :, patches(c)]

            @pl.when(other(d, e))
            def _():
                pltpu.make_async_remote_copy(
                    src_ref=src, dst_ref=dst, send_sem=ga_send.at[c], recv_sem=ga_recv.at[c],
                    device_id=(d, e), device_id_type=MESH).start()

            @pl.when(jnp.logical_not(other(d, e)))
            def _():
                pltpu.make_async_copy(src, dst, ga_recv.at[c]).start()

            return 0

        lax.fori_loop(0, 16, ga_go, 0)

    key_at = lax.broadcasted_iota(jnp.int32, (128, 128), 0)
    query_at = lax.broadcasted_iota(jnp.int32, (128, 128), 1)
    seen = jnp.logical_and(query_at >= key_at, (query_at >= 64) == (key_at >= 64))

    def widen(src):
        def step(i, _):
            x32[pl.ds(pl.multiple_of(i * 128, 128), 128)] = src[i].reshape(128, HD).astype(F32)
            return 0

        lax.fori_loop(0, 16, step, 0)

    def pair_of(p):
        a = x32[pl.ds(2 * p, 64, stride=32), :]
        b = x32[pl.ds(2 * p + 1, 64, stride=32), :]
        return jnp.concatenate([a, b], axis=0).astype(BF16)

    for n, (dst, out) in enumerate(((rq, qt), (rk, kt), (rv, vt))):
        pltpu.make_async_copy(dst, dst, in_recv.at[n]).wait()
        widen(dst)

        def regroup(p, _, out=out):
            out[p] = pair_of(p)
            return 0

        lax.fori_loop(0, 16, regroup, 0)

    def soft(p, _):
        scores = jnp.where(seen, dot(kt[p], qt[p], NT) * inv_root, -1e30)
        e = jnp.exp(scores - jnp.max(scores, axis=0, keepdims=True))
        pt[p] = e / jnp.sum(e, axis=0, keepdims=True)
        return 0

    lax.fori_loop(0, 16, soft, 0)

    outs = (oq, ok, ov)

    def out_copy(n, c, d):
        return pltpu.make_async_remote_copy(
            src_ref=so.at[n, d, :, patches(c)], dst_ref=outs[n].at[0, :, patches(c), lanes(s)],
            send_sem=o_send.at[n], recv_sem=o_recv.at[n],
            device_id=(dp, d), device_id_type=MESH)

    for c in range(2):
        part = rg.at[:, :, patches(c)]
        pltpu.make_async_copy(part, part, ga_recv.at[c]).wait()

        def widen_g(i, _, c=c):
            for f in range(4):
                x32[pl.ds(pl.multiple_of(i * 128 + f * 32 + c * 16, 16), 16)] = rg[i, f, c * 16 : c * 16 + 16].astype(F32)
            return 0

        lax.fori_loop(0, 16, widen_g, 0)

        def place(n, p, val):
            o32[n, pl.ds(2 * p, 64, stride=32), :] = val[:64]
            o32[n, pl.ds(2 * p + 1, 64, stride=32), :] = val[64:]

        def value_grad(p, _):
            gp = pair_of(p)
            gt[p] = gp
            place(2, p, dot(pt[p].astype(BF16), gp, NN))
            return 0

        def score_grads(p, _):
            prob = pt[p]
            grad_prob = dot(vt[p], gt[p], NT)
            delta = jnp.sum(prob.astype(BF16).astype(F32) * grad_prob, axis=0, keepdims=True)
            ds = (prob * (grad_prob - delta) * inv_root).astype(BF16)
            vt[p] = ds
            place(1, p, dot(ds, qt[p], NN))
            return 0

        def query_grad(p, _):
            place(0, p, dot(vt[p], kt[p], TN))
            return 0

        def give(n, c=c):
            def narrow(i, _):
                for f in range(4):
                    rows = pl.ds(pl.multiple_of(i * 128 + f * 32 + c * 16, 16), 16)
                    so[n, i, f, c * 16 : c * 16 + 16] = o32[n, rows, :].astype(BF16)
                return 0

            lax.fori_loop(0, 16, narrow, 0)
            pltpu.make_async_copy(
                so.at[n, s, :, patches(c)], outs[n].at[0, :, patches(c), lanes(s)], o_recv.at[n]).start()

            def out_go(i, _):
                out_copy(n, c, lax.rem(s + i, 16)).start()
                return 0

            lax.fori_loop(1, 16, out_go, 0)

        lax.fori_loop(c * 8, c * 8 + 8, value_grad, 0)
        give(2)
        lax.fori_loop(c * 8, c * 8 + 8, score_grads, 0)
        give(1)
        lax.fori_loop(c * 8, c * 8 + 8, query_grad, 0)
        give(0)

    for n, (src, dst) in enumerate(pairs):
        part = src.at[0, :, :, pl.ds(0, 15 * HD)]
        pltpu.make_async_copy(part, part, in_send.at[n]).wait()
    for step, way, h in hops:
        z_copy(way, h, step).wait_send()
    for copy in (to_right, to_left, to_twin, on_right, on_left, twin_before, twin_after, twin_near, twin_far):
        copy.wait_send()

    def drain(ref, sem):
        pltpu.make_async_copy(ref, ref, sem).wait()

    @pl.when(own)
    def _():
        drain(wt.at[pl.ds(0, 224)], w_send)
        for c in range(2):
            drain(rg.at[pl.ds(0, 14), :, patches(c)], ga_send.at[c])

    @pl.when(jnp.logical_not(own))
    def _():
        drain(wt.at[pl.ds(0, 256)], w_send)
        for c in range(2):
            drain(rg.at[:, :, patches(c)], ga_send.at[c])

    for n in range(3):
        drain(so.at[n, pl.ds(0, 15)], o_send.at[n])
        drain(outs[n], o_recv.at[n])


def put(a, b, c, oa, ob, oc, sem):
    copies = [pltpu.make_async_copy(src, dst, sem.at[n]) for n, (src, dst) in enumerate(((a, oa), (b, ob), (c, oc)))]
    for copy in copies:
        copy.start()
    for copy in copies:
        copy.wait()


def body(query_saved, key_saved, value_saved, grad_block, out_weight):
    shape = jax.ShapeDtypeStruct(query_saved.shape, BF16)
    anywhere = pl.BlockSpec(memory_space=pl.ANY)
    dma = pltpu.SemaphoreType.DMA
    near = pltpu.VMEM(query_saved.shape, BF16)
    grads = pl.pallas_call(
        kernel,
        out_shape=(near, near, near),
        in_specs=[anywhere] * 5,
        out_specs=(anywhere,) * 3,
        scratch_shapes=[
            *[pltpu.VMEM((16, 4, 32, HD), BF16)] * 4,
            pltpu.VMEM((8, 4, 32, 2048), BF16),
            pltpu.VMEM((2048, 256), BF16),
            pltpu.VMEM((2, 8, 4, 32, HD), BF16),
            pltpu.VMEM((2048, HD), F32),
            *[pltpu.VMEM((16, 128, HD), BF16)] * 4,
            pltpu.VMEM((16, 128, 128), F32),
            pltpu.VMEM((3, 2048, HD), F32),
            pltpu.VMEM((3, 16, 4, 32, HD), BF16),
            dma((3,)), dma((3,)),
            dma, dma,
            dma((2, 2, 4)), dma((2, 2, 4)),
            dma((10,)), dma((10,)),
            dma((2,)), dma((2,)),
            dma((3,)), dma((3,)),
        ],
        compiler_params=pltpu.CompilerParams(
            collective_id=0, has_side_effects=True, vmem_limit_bytes=60 * 1024 * 1024),
    )(query_saved, key_saved, value_saved, grad_block, out_weight.T)
    return pl.pallas_call(
        put, out_shape=(shape, shape, shape), in_specs=[pl.BlockSpec(memory_space=pltpu.VMEM)] * 3,
        out_specs=(anywhere,) * 3, scratch_shapes=[dma((3,))],
    )(*[pltpu.with_memory_space_constraint(a, pltpu.VMEM) for a in grads])


def solution(mesh):
    spec = P("dp", "seq", None, None)
    return jax.shard_map(
        body, mesh=mesh, in_specs=(spec, spec, spec, spec, P("seq", "dp")), out_specs=(spec, spec, spec), check_vma=False)
```
